32 devices in a mesh: grp: 2 (over y), row: 4 (over z), col: 2 (over x), sub: 2 (over core).
Axes of the slice: x: 2, y: 2, z: 4, core: 2. Of those that a mesh axis runs over, the one named last changes fastest.
Arguments:
- sigma_parent: float32 [6, 4, 256, 6, 2, 256], P('grp', 'row', 'sub', None, 'col'), parts along dimension 0, may hold values from -10 to 10
- panel: float32 [4, 4, 256, 256], P(('grp', 'col'), 'row', 'sub'), parts along dimension 0, may hold values from -0.6 to 0.6
- diag_factor: float32 [4, 256, 256], P(('grp', 'col')), parts along dimension 0, may hold values from -1 to 3, as said below
- frontier: int32 [4, 4], P('grp'), parts along dimension 0, may hold values from 0 to 11, as said below
Outputs:
- sigma_cross: float32 [4, 4, 256, 256], P(('grp', 'col'), 'row', 'sub'), parts along dimension 0
- sigma_diag: float32 [4, 256, 256], P(('grp', 'col')), parts along dimension 0
The draws below stay inside these ranges and needn't reach their ends.
There are 2 independent parts, one for each index of `grp`. The reference program is written for one: setup_inputs(seed, part) draws one part's arguments, and reference() takes and returns one part's arrays. A program takes and returns all parts, laid end to end along the dimension named above; each array names one. Nothing has to cross between parts.
Inputs may be any that keep to these rules, and one draw needn't show every extreme that they name: `frontier`: each row holds 4 different parent block numbers in increasing order; in each row at most 3 of them share one remainder modulo the number of block-column owners, and exactly 3 do for some remainder. `diag_factor`: lower triangular, every diagonal entry at least 1.
All inputs are finite; a program needn't handle non-finite values.
Results may differ from the reference program's by a relative error of at most 0.000071.
Values sent between devices are 32-bit elements; how exact they have to be, the bound alone decides.
A program may use at most 64 MiB of HBM per device.

```python
import math
import jax
import jax.numpy as jnp
from jax import lax

BLOCK = 256
PAR_ROWS = 3
KIDS_COL = 1
PARENT = 12
PAR_COLS = 6
FRONT = 4
CHILDREN = 2


def draw_sigma_parent(key, part):
    key = jax.random.fold_in(key, 11)
    order_len = PARENT * BLOCK
    first_key = jax.random.fold_in(key, 0)
    base = jax.random.normal(first_key, (order_len, order_len), jnp.float32)
    mixed = (base + base.T) * (0.35 / math.sqrt(order_len))
    line = lax.iota(jnp.int32, order_len)
    mixed = mixed + (line[:, None] == line[None, :]).astype(jnp.float32)
    return mixed.reshape(PAR_ROWS, PARENT // PAR_ROWS, BLOCK, PAR_COLS, PARENT // PAR_COLS, BLOCK)


def draw_diag_factor(key, part):
    key = jax.random.fold_in(key, 12)
    first_key, second_key = jax.random.split(key)
    lower_part = jax.random.normal(first_key, (CHILDREN, BLOCK, BLOCK), jnp.float32) * (0.5 / math.sqrt(BLOCK))
    diagonal = jax.random.uniform(second_key, (CHILDREN, BLOCK), jnp.float32, 1.5, 3.0)
    line = lax.iota(jnp.int32, BLOCK)
    strict = (line[:, None] > line[None, :]).astype(jnp.float32)
    on_diag = (line[:, None] == line[None, :]).astype(jnp.float32)
    return lower_part * strict[None] + diagonal[:, :, None] * on_diag[None]


def child_struct(child_key):
    col_total = CHILDREN // KIDS_COL
    mean_count = FRONT // col_total
    first_key, second_key, third_key = jax.random.split(child_key, 3)
    col_order = jax.random.permutation(first_key, col_total)
    flips = jax.random.randint(second_key, (col_total // 2,), 0, 2).astype(jnp.int32)
    flips = flips.at[0].set(1)
    pair_sign = jnp.stack([flips, -flips], axis=1).reshape(col_total)
    counts = jnp.zeros((col_total,), jnp.int32).at[col_order].set(mean_count + pair_sign)
    rank_keys = jax.random.split(third_key, col_total)
    ranks = jax.vmap(lambda sub_key: jax.random.permutation(sub_key, PAR_COLS))(rank_keys)
    chosen = (ranks.T < counts[None, :]).reshape(PARENT).astype(jnp.int32)
    score = (1 - chosen) * PARENT + lax.iota(jnp.int32, PARENT)
    return jnp.argsort(score)[:FRONT].astype(jnp.int32)


def draw_frontier(key, part):
    key = jax.random.fold_in(key, 13)
    child_keys = jax.random.split(key, CHILDREN)
    return jax.vmap(child_struct)(child_keys)


def block_scale(key, dims, cuts, least, largest):
    def one(dim, shards_of):
        heights = jax.random.uniform(jax.random.fold_in(jax.random.fold_in(key, 6), dim), (shards_of,), jnp.float32, least / len(cuts), largest / len(cuts))
        return jnp.repeat(jnp.exp(heights), dims[dim] // shards_of).reshape((-1,) + (1,) * (len(dims) - dim - 1))

    gain = one(*cuts[0])
    for cut in cuts[1:]:
        gain = gain * one(*cut)
    return gain


def bell_draw(stream_key, extent, width, reach, shards=(), kind=jnp.bfloat16):
    loudness = block_scale(stream_key, extent, shards, -0.22, 0.18) if shards else 1.0
    drawn = jax.random.normal(stream_key, extent, jnp.float32) * width * loudness
    return jnp.minimum(jnp.maximum(drawn, -reach), reach).astype(kind)


def setup_inputs(seed: int = 0, part: int = 0) -> dict:
    splits = jax.random.split(jax.random.key(seed), 5)
    own_keys = jax.random.split(jax.random.fold_in(splits[4], part), 5)
    return {
        "sigma_parent": draw_sigma_parent(jax.random.fold_in(jax.random.fold_in(splits[4], part), 71), part),
        "panel": bell_draw(own_keys[1], (CHILDREN, FRONT, BLOCK, BLOCK), 0.1, 0.6, ((0, 2), (1, 4), (2, 2)), jnp.float32),
        "diag_factor": draw_diag_factor(jax.random.fold_in(jax.random.fold_in(splits[4], part), 71), part),
        "frontier": draw_frontier(jax.random.fold_in(jax.random.fold_in(splits[4], part), 71), part),
    }


HIGHEST = lax.Precision.HIGHEST

def one_child(parent, items):
    panel_blocks, factor, struct = items
    identity = jnp.eye(BLOCK, dtype=jnp.float32)
    inverse = lax.linalg.triangular_solve(factor, identity, left_side=True, lower=True)
    update = jnp.dot(panel_blocks.reshape(FRONT * BLOCK, BLOCK), inverse, precision=HIGHEST)
    chosen = parent[struct][:, :, struct]
    cross = -jnp.dot(chosen.reshape(FRONT * BLOCK, FRONT * BLOCK), update, precision=HIGHEST)
    diag_out = jnp.dot(inverse.T, inverse, precision=HIGHEST) - jnp.dot(update.T, cross, precision=HIGHEST)
    return (cross.reshape(FRONT, BLOCK, BLOCK), diag_out)

def reference(sigma_parent, panel, diag_factor, frontier):
    parent = sigma_parent.reshape(PARENT, BLOCK, PARENT, BLOCK)
    sigma_cross, sigma_diag = lax.map(lambda items: one_child(parent, items), (panel, diag_factor, frontier))
    return (sigma_cross, sigma_diag)
```

```python
import functools
import jax
import jax.numpy as jnp
from jax import lax
from jax.experimental import pallas as pl
from jax.experimental.pallas import tpu as pltpu
from jax.sharding import PartitionSpec as P

HIGHEST = lax.Precision.HIGHEST
MESH = pl.DeviceIdType.MESH
F32 = jnp.float32
BF16 = jnp.bfloat16


def split(x):
    hi = x.astype(BF16)
    return hi, (x - hi.astype(F32)).astype(BF16)


def dot3(a, b, dims=((1,), (0,))):
    def one(x, y):
        return lax.dot_general(x, y, (dims, ((), ())), preferred_element_type=F32)

    return one(a[0], b[0]) + (one(a[0], b[1]) + one(a[1], b[0]))


def dot6(a, b):
    return jnp.dot(a, b, precision=HIGHEST, preferred_element_type=F32)


def invert_lower(tri):
    size = tri.shape[0]
    row = lax.broadcasted_iota(jnp.int32, (size, size), 0)
    col = lax.broadcasted_iota(jnp.int32, (size, size), 1)
    on_diag = row == col
    only = jnp.where(on_diag, tri, 0.0)
    by_col = 1.0 / jnp.sum(only, axis=0, keepdims=True)
    by_row = 1.0 / jnp.sum(only, axis=1, keepdims=True)

    def below(m):
        same = (row // (2 * m)) == (col // (2 * m))
        return same & ((row // m) % 2 == 1) & ((col // m) % 2 == 0)

    inv = jnp.where(on_diag, by_row, 0.0) - jnp.where(below(1), tri * by_row * by_col, 0.0)
    m = 2
    while m < size:
        inv = inv - dot6(inv, dot6(jnp.where(below(m), tri, 0.0), inv))
        m *= 2
    return inv


def kernel(R, C, *refs):
    front, parent, panel, factor, cross_out, diag_out = refs[:6]
    pk = refs[6 : 6 + C]
    (s_hi, s_lo, inv_hi, inv_lo, ysend, yrecv, w, wsend, wrecv, macc, mrecv, mhalf, mpart, gall,
     main_s, main_r, sub_s, sub_r, y_s, y_r, w_s, w_r, ms_s, ms_r, m_s, m_r, g_s, g_r, gs_s, gs_r) = refs[6 + C :]
    half = panel.shape[0]
    width = panel.shape[1]
    par_rows = w.shape[0]
    front_len = front.shape[1]
    slots = front_len // C + 1
    piece = half // R
    r = lax.axis_index("row")
    c = lax.axis_index("col")
    s = lax.axis_index("sub")
    other = 1 - s

    def rowat(d):
        return lax.rem(r + d + R, R)

    def colat(e):
        return lax.rem(c + e + C, C)

    barrier = pltpu.get_barrier_semaphore()
    for d in range(1, R):
        pl.semaphore_signal(barrier, inc=1, device_id={"row": rowat(d)}, device_id_type=MESH)
    for e in range(1, C):
        pl.semaphore_signal(barrier, inc=1, device_id={"col": colat(e)}, device_id_type=MESH)
    pl.semaphore_signal(barrier, inc=1, device_id={"sub": other}, device_id_type=MESH)
    pl.semaphore_wait(barrier, R - 1 + C - 1 + 1)

    started = []

    def send(src, dst, ssem, rsem, dev):
        copy = pltpu.make_async_remote_copy(
            src_ref=src, dst_ref=dst, send_sem=ssem, recv_sem=rsem, device_id=dev, device_id_type=MESH
        )
        copy.start()
        started.append(copy)

    def arrived(dst, ssem, rsem):
        pltpu.make_async_remote_copy(
            src_ref=dst, dst_ref=dst, send_sem=ssem, recv_sem=rsem, device_id={"sub": other}, device_id_type=MESH
        ).wait_recv()

    far_first = sorted(range(1, R), key=lambda d: abs(d - R / 2))
    near_first = far_first[::-1]

    pk[0][r, s] = panel[...]
    own = pk[0].at[r, s]
    for d in far_first:
        send(own, own, main_s.at[d], main_r.at[d], {"row": rowat(d)})
    for e in range(1, C):
        send(own, pk[e].at[r, s], main_s.at[e * R], main_r.at[e * R], {"col": colat(e)})
    send(own, own, sub_s.at[0], sub_r.at[0], {"sub": other})

    for j in range(parent.shape[0]):
        hi, lo = split(parent[j])
        s_hi[j] = hi
        s_lo[j] = lo

    def take_row(d):
        block = pk[0].at[rowat(-d), s]
        arrived(block, main_s.at[d], main_r.at[d])
        for e in range(1, C):
            key = e * R + d
            send(block, pk[e].at[rowat(-d), s], main_s.at[key], main_r.at[key], {"col": colat(e)})
        send(block, block, sub_s.at[d], sub_r.at[d], {"sub": other})

    def take_col(e, d):
        block = pk[e].at[rowat(-d), s]
        key = e * R + d
        arrived(block, main_s.at[key], main_r.at[key])
        send(block, block, sub_s.at[key], sub_r.at[key], {"sub": other})

    def take_sub(e, d):
        key = e * R + d
        arrived(pk[e].at[rowat(-d), other], sub_s.at[key], sub_r.at[key])

    for d in near_first:
        take_row(d)

    h = width // 2
    tri = factor[...]
    top = invert_lower(tri[:h, :h])
    low = invert_lower(tri[h:, h:])
    corner = -dot6(low, dot6(tri[h:, :h], top))
    inverse = jnp.concatenate(
        [jnp.concatenate([top, jnp.zeros((h, h), F32)], axis=1), jnp.concatenate([corner, low], axis=1)], axis=0
    )
    hi, lo = split(inverse)
    inv_hi[...] = hi
    inv_lo[...] = lo

    for d in [0] + near_first:
        for e in range(1, C):
            take_col(e, d)

    def product(e):
        kid = colat(-e)
        count = jnp.int32(0)
        which = [jnp.int32(0)] * slots
        column = [jnp.int32(0)] * slots
        for b in range(front_len):
            f = front[kid, b]
            hit = lax.rem(f, C) == c
            for m in range(slots):
                here = hit & (count == m)
                which[m] = jnp.where(here, b, which[m])
                column[m] = jnp.where(here, lax.div(f, C), column[m])
            count = count + hit.astype(jnp.int32)
        total = None
        for m in range(slots):
            used = jnp.where(count > m, 1.0, 0.0).astype(F32)
            block = pk[e][which[m]].reshape(2 * half, width) * used
            term = dot3((s_hi[column[m]], s_lo[column[m]]), split(block))
            total = term if total is None else total + term
        return total.reshape(par_rows, half, width)

    for d in range(R):
        take_sub(0, d)
    w[...] = product(0)
    for e in range(1, C):
        for d in range(R):
            take_sub(e, d)
        ysend[e - 1] = product(e)
        send(ysend.at[e - 1], yrecv.at[e - 1], y_s.at[e - 1], y_r.at[e - 1], {"col": colat(-e)})
    for e in range(1, C):
        arrived(yrecv.at[e - 1], y_s.at[e - 1], y_r.at[e - 1])
        w[...] = w[...] + yrecv[e - 1]

    lhs = []
    for p in range(par_rows):
        which = jnp.int32(0)
        used = jnp.float32(0.0)
        for a in range(front_len):
            here = front[c, a] == p * R + r
            which = jnp.where(here, a, which)
            used = jnp.where(here, 1.0, used)
        lhs.append(pk[0][which, s] * used)
    lhs = jnp.concatenate(lhs, axis=0)
    macc[...] = dot3(split(lhs), split(w[...].reshape(par_rows * half, width)), ((0,), (0,))).reshape(2, half, width)
    send(macc.at[other], mrecv, ms_s.at[0], ms_r.at[0], {"sub": other})

    for d in far_first + [0]:
        wsend[d] = w[lax.div(front[c, rowat(d)], R)]
        if d:
            send(wsend.at[d], wrecv.at[d], w_s.at[d], w_r.at[d], {"row": rowat(d)})
    wrecv[0] = wsend[0]

    arrived(mrecv, ms_s.at[0], ms_r.at[0])
    mhalf[...] = (macc[s] + mrecv[...]).reshape(R, piece, width)
    for d in far_first:
        send(mhalf.at[rowat(d)], mpart.at[d], m_s.at[d], m_r.at[d], {"row": rowat(d)})
    total = mhalf[r]
    for d in near_first:
        arrived(mpart.at[d], m_s.at[d], m_r.at[d])
        total = total + mpart[d]
    row = lax.broadcasted_iota(jnp.int32, (piece, width), 0) + (s * half + r * piece)
    col = lax.broadcasted_iota(jnp.int32, (piece, width), 1)
    total = total + jnp.where(row == col, 1.0, 0.0)
    inv_pair = (inv_hi[...], inv_lo[...])
    gall[s, r] = dot3(split(total), inv_pair)
    mine = gall.at[s, r]
    for d in far_first:
        send(mine, mine, g_s.at[d], g_r.at[d], {"row": rowat(d)})
    send(mine, mine, gs_s.at[0], gs_r.at[0], {"sub": other})
    for d in near_first:
        block = gall.at[s, rowat(-d)]
        arrived(block, g_s.at[d], g_r.at[d])
        send(block, block, gs_s.at[d], gs_r.at[d], {"sub": other})

    for d in near_first:
        arrived(wrecv.at[d], w_s.at[d], w_r.at[d])
    owner = lax.rem(front[c, r], R)
    picked = wrecv[lax.rem(r - owner + R, R)]
    cross_out[...] = -dot3(split(picked), inv_pair)

    for d in range(R):
        arrived(gall.at[other, rowat(-d)], gs_s.at[d], gs_r.at[d])
    diag_out[...] = dot3(inv_pair, split(gall[...].reshape(2 * half, width)), ((0,), (0,)))

    for copy in started:
        copy.wait_send()


def per_device(R, C, sigma_parent, panel, diag_factor, frontier):
    half, width = panel.shape[2:]
    par_rows, par_cols = sigma_parent.shape[0], sigma_parent.shape[3]
    front_len = frontier.shape[1]
    parent = sigma_parent.reshape(par_rows, half, par_cols, width)
    parent = parent.transpose(2, 0, 1, 3).reshape(par_cols, par_rows * half, width)
    vm = pltpu.VMEM
    dma = pltpu.SemaphoreType.DMA
    side = max(C - 1, 1)
    piece = half // R
    scratch = [vm((front_len, 2, half, width), F32) for _ in range(C)] + [
        vm((par_cols, par_rows * half, width), BF16),
        vm((par_cols, par_rows * half, width), BF16),
        vm((width, width), BF16),
        vm((width, width), BF16),
        vm((side, par_rows, half, width), F32),
        vm((side, par_rows, half, width), F32),
        vm((par_rows, half, width), F32),
        vm((R, half, width), F32),
        vm((R, half, width), F32),
        vm((2, half, width), F32),
        vm((half, width), F32),
        vm((R, piece, width), F32),
        vm((R, piece, width), F32),
        vm((2, R, piece, width), F32),
        dma((R * C,)), dma((R * C,)), dma((R * C,)), dma((R * C,)),
        dma((side,)), dma((side,)), dma((R,)), dma((R,)), dma((1,)), dma((1,)),
        dma((R,)), dma((R,)), dma((R,)), dma((R,)), dma((R,)), dma((R,)),
    ]
    spec = pl.BlockSpec(memory_space=pltpu.VMEM)
    cross, diag = pl.pallas_call(
        functools.partial(kernel, R, C),
        out_shape=(jax.ShapeDtypeStruct((half, width), F32), jax.ShapeDtypeStruct((width, width), F32)),
        in_specs=[pl.BlockSpec(memory_space=pltpu.SMEM), spec, spec, spec],
        out_specs=(spec, spec),
        scratch_shapes=scratch,
        compiler_params=pltpu.CompilerParams(
            collective_id=0, has_side_effects=True, vmem_limit_bytes=(24 if C == 2 else 58) * 2**20
        ),
    )(frontier, parent, panel.reshape(half, width), diag_factor.reshape(width, width))
    return cross.reshape(panel.shape), diag.reshape(diag_factor.shape)


def solution(mesh):
    in_specs = (
        P("grp", "row", "sub", None, "col", None),
        P(("grp", "col"), "row", "sub", None),
        P(("grp", "col"), None, None),
        P("grp", None),
    )
    out_specs = (P(("grp", "col"), "row", "sub", None), P(("grp", "col"), None, None))
    return jax.shard_map(
        functools.partial(per_device, mesh.shape["row"], mesh.shape["col"]),
        mesh=mesh, in_specs=in_specs, out_specs=out_specs, check_vma=False,
    )
```

```python
import functools
import jax
import jax.numpy as jnp
from jax import lax
from jax.experimental import pallas as pl
from jax.experimental.pallas import tpu as pltpu
from jax.sharding import PartitionSpec as P

HIGHEST = lax.Precision.HIGHEST
MESH = pl.DeviceIdType.MESH
F32 = jnp.float32
BF16 = jnp.bfloat16


def split(x):
    hi = x.astype(BF16)
    return hi, (x - hi.astype(F32)).astype(BF16)


def dot3(a, b, dims=((1,), (0,))):
    def one(x, y):
        return lax.dot_general(x, y, (dims, ((), ())), preferred_element_type=F32)

    return one(a[0], b[0]) + (one(a[0], b[1]) + one(a[1], b[0]))


def dot6(a, b):
    return jnp.dot(a, b, precision=HIGHEST, preferred_element_type=F32)


def invert_steps(tri):
    size = tri.shape[0]
    row = lax.broadcasted_iota(jnp.int32, (size, size), 0)
    col = lax.broadcasted_iota(jnp.int32, (size, size), 1)
    on_diag = row == col
    only = jnp.where(on_diag, tri, 0.0)
    by_col = 1.0 / jnp.sum(only, axis=0, keepdims=True)
    by_row = 1.0 / jnp.sum(only, axis=1, keepdims=True)

    def below(m):
        same = (row // (2 * m)) == (col // (2 * m))
        return same & ((row // m) % 2 == 1) & ((col // m) % 2 == 0)

    inv = jnp.where(on_diag, by_row, 0.0) - jnp.where(below(1), tri * by_row * by_col, 0.0)
    yield inv
    m = 2
    while m < size:
        inv = inv - dot6(inv, dot6(jnp.where(below(m), tri, 0.0), inv))
        m *= 2
        yield inv


CH = 2


def kernel(R, C, *refs):
    refs = list(refs)
    front, parent, panel, factor, cross_out, diag_out = refs[:6]
    del refs[:6]
    pk = [[refs.pop(0) for _ in range(CH)] for _ in range(C)]
    w = [refs.pop(0) for _ in range(CH)]
    wsend = [refs.pop(0) for _ in range(CH)]
    wrecv = [refs.pop(0) for _ in range(CH)]
    (s_hi, s_lo, inv_hi, inv_lo, ysend, yrecv, macc, mrecv, mhalf, mpart, gall,
     z_s, z_r, x_s, x_r, sub_s, sub_r, y_s, y_r, w_s, w_r, ms_s, ms_r, m_s, m_r, g_s, g_r, gs_s, gs_r) = refs
    half = panel.shape[0]
    width = panel.shape[1]
    wide = width // CH
    par_rows = w[0].shape[0]
    front_len = front.shape[1]
    slots = front_len // C + 1
    piece = half // R
    r = lax.axis_index("row")
    c = lax.axis_index("col")
    s = lax.axis_index("sub")
    other = 1 - s

    def rowat(d):
        return lax.rem(r + d + R, R)

    def colat(e):
        return lax.rem(c + e + C, C)

    barrier = pltpu.get_barrier_semaphore()
    for d in range(1, R):
        pl.semaphore_signal(barrier, inc=1, device_id={"row": rowat(d)}, device_id_type=MESH)
    for e in range(1, C):
        pl.semaphore_signal(barrier, inc=1, device_id={"col": colat(e)}, device_id_type=MESH)
    pl.semaphore_signal(barrier, inc=1, device_id={"sub": other}, device_id_type=MESH)
    pl.semaphore_wait(barrier, R - 1 + C - 1 + 1)

    started = []

    def remote(src, dst, ssem, rsem, dev):
        return pltpu.make_async_remote_copy(
            src_ref=src, dst_ref=dst, send_sem=ssem, recv_sem=rsem, device_id=dev, device_id_type=MESH
        )

    def send(src, dst, ssem, rsem, dev, cond=None):
        def go():
            remote(src, dst, ssem, rsem, dev).start()

        def done():
            remote(src, dst, ssem, rsem, dev).wait_send()

        when(cond, go)
        started.append((cond, done))

    def when(cond, body):
        if cond is None:
            body()
        else:
            pl.when(cond)(body)

    def arrived(dst, ssem, rsem):
        remote(dst, dst, ssem, rsem, {"sub": other}).wait_recv()

    far_first = sorted(range(1, R), key=lambda d: abs(d - R / 2))
    near_first = far_first[::-1]

    def key(way, t, ch):
        return (way * R + t) * CH + ch

    keys = 2 * R * CH

    def source(way, t):
        return r - t if way == 0 else r + t

    def from_row(way, t):
        if t == 0:
            return None
        return r >= t if way == 0 else r + t <= R - 1

    def both(a, b):
        return b if a is None else a & b

    def pass_on(way, t, ch):
        here = from_row(way, t)
        block = pk[0][ch].at[source(way, t), s]
        if t + 1 < R:
            for side in (0, 1) if t == 0 else (way,):
                k = key(side, t + 1, ch)
                inside = r < R - 1 if side == 0 else r > 0
                send(block, block, z_s.at[k], z_r.at[k], {"row": r + 1 if side == 0 else r - 1}, both(here, inside))
        k = key(way, t, ch)
        for e in range(1, C):
            q = (e - 1) * keys + k
            send(block, pk[e][ch].at[source(way, t), s], x_s.at[q], x_r.at[q], {"col": colat(e)}, here)
        send(block, block, sub_s.at[k], sub_r.at[k], {"sub": other}, here)

    def take_row(way, t, ch):
        k = key(way, t, ch)
        when(from_row(way, t), lambda: arrived(pk[0][ch].at[source(way, t), s], z_s.at[k], z_r.at[k]))
        pass_on(way, t, ch)

    def take_col(e, way, t, ch):
        q = (e - 1) * keys + key(way, t, ch)
        here = from_row(way, t)
        block = pk[e][ch].at[source(way, t), s]
        when(here, lambda: arrived(block, x_s.at[q], x_r.at[q]))
        q += keys
        send(block, block, sub_s.at[q], sub_r.at[q], {"sub": other}, here)

    def take_sub(e, way, t, ch):
        q = e * keys + key(way, t, ch)
        when(from_row(way, t), lambda: arrived(pk[e][ch].at[source(way, t), other], sub_s.at[q], sub_r.at[q]))

    h = width // 2
    tri = factor[...]
    steps = [invert_steps(tri[:h, :h]), invert_steps(tri[h:, h:])]
    blocks = [None, None]

    def advance(count=1):
        for _ in range(count):
            for i in range(2):
                blocks[i] = next(steps[i], blocks[i])

    for ch in range(CH):
        pk[0][ch][r, s] = panel[:, ch * wide : (ch + 1) * wide]
        pass_on(0, 0, ch)

    for j in range(parent.shape[0]):
        hi, lo = split(parent[j])
        s_hi[j] = hi
        s_lo[j] = lo

    for t in range(1, R):
        for ch in range(CH):
            take_row(0, t, ch)
            take_row(1, t, ch)
        for ch in range(CH):
            for e in range(1, C):
                for way in (0,) if t == 1 else (0, 1):
                    take_col(e, way, t - 1, ch)
        if t < 3:
            advance()

    def product(e, ch):
        kid = colat(-e)
        count = jnp.int32(0)
        which = [jnp.int32(0)] * slots
        column = [jnp.int32(0)] * slots
        for b in range(front_len):
            f = front[kid, b]
            hit = lax.rem(f, C) == c
            for m in range(slots):
                here = hit & (count == m)
                which[m] = jnp.where(here, b, which[m])
                column[m] = jnp.where(here, lax.div(f, C), column[m])
            count = count + hit.astype(jnp.int32)
        total = None
        for m in range(slots):
            used = jnp.where(count > m, 1.0, 0.0).astype(F32)
            block = pk[e][ch][which[m]].reshape(2 * half, wide) * used
            term = dot3((s_hi[column[m]], s_lo[column[m]]), split(block))
            total = term if total is None else total + term
        return total.reshape(par_rows, half, wide)

    ways = [(0, 0)] + [(way, t) for t in range(1, R) for way in (0, 1)]
    for ch in range(CH):
        for e in range(1, C):
            for way in (0, 1) if R > 1 else ():
                take_col(e, way, R - 1, ch)
    for ch in range(CH):
        for e in range(1, C):
            for way, t in ways:
                take_sub(e, way, t, ch)
            n = (e - 1) * CH + ch
            ysend[n] = product(e, ch)
            send(ysend.at[n], yrecv.at[n], y_s.at[n], y_r.at[n], {"col": colat(-e)})
    for ch in range(CH):
        for way, t in ways:
            take_sub(0, way, t, ch)
    for ch in range(CH):
        w[ch][...] = product(0, ch)

    lhs = []
    for p in range(par_rows):
        which = jnp.int32(0)
        used = jnp.float32(0.0)
        for a in range(front_len):
            here = front[c, a] == p * R + r
            which = jnp.where(here, a, which)
            used = jnp.where(here, 1.0, used)
        lhs.append(jnp.concatenate([pk[0][ch][which, s] for ch in range(CH)], axis=1) * used)
    lhs = split(jnp.concatenate(lhs, axis=0))
    advance(3)

    def rows_out(ch):
        for e in range(1, C):
            n = (e - 1) * CH + ch
            arrived(yrecv.at[n], y_s.at[n], y_r.at[n])
            w[ch][...] = w[ch][...] + yrecv[n]
        macc[ch] = dot3(lhs, split(w[ch][...].reshape(par_rows * half, wide)), ((0,), (0,))).reshape(2, half, wide)
        send(macc.at[ch, other], mrecv.at[ch], ms_s.at[ch], ms_r.at[ch], {"sub": other})
        for d in far_first + [0]:
            wsend[ch][d] = w[ch][lax.div(front[c, rowat(d)], R)]
            if d:
                k = ch * R + d
                send(wsend[ch].at[d], wrecv[ch].at[d], w_s.at[k], w_r.at[k], {"row": rowat(d)})
        wrecv[ch][0] = wsend[ch][0]

    def diag_out_part(ch):
        arrived(mrecv.at[ch], ms_s.at[ch], ms_r.at[ch])
        mhalf[ch] = (macc[ch, s] + mrecv[ch]).reshape(R, piece, wide)
        for d in far_first:
            k = ch * R + d
            send(mhalf.at[ch, rowat(d)], mpart.at[ch, d], m_s.at[k], m_r.at[k], {"row": rowat(d)})

    for ch in range(CH):
        rows_out(ch)
        diag_out_part(ch)

    advance(8)
    top, low = blocks
    corner = -dot6(low, dot6(tri[h:, :h], top))
    inverse = jnp.concatenate(
        [jnp.concatenate([top, jnp.zeros((h, h), F32)], axis=1), jnp.concatenate([corner, low], axis=1)], axis=0
    )
    hi, lo = split(inverse)
    inv_hi[...] = hi
    inv_lo[...] = lo
    inv_pair = (inv_hi[...], inv_lo[...])

    total = []
    for ch in range(CH):
        part = mhalf[ch, r]
        for d in near_first:
            k = ch * R + d
            arrived(mpart.at[ch, d], m_s.at[k], m_r.at[k])
            part = part + mpart[ch, d]
        total.append(part)
    total = jnp.concatenate(total, axis=1)
    row = lax.broadcasted_iota(jnp.int32, (piece, width), 0) + (s * half + r * piece)
    col = lax.broadcasted_iota(jnp.int32, (piece, width), 1)
    total = total + jnp.where(row == col, 1.0, 0.0)
    gall[s, r] = dot3(split(total), inv_pair)
    mine = gall.at[s, r]
    for d in far_first:
        send(mine, mine, g_s.at[d], g_r.at[d], {"row": rowat(d)})
    send(mine, mine, gs_s.at[0], gs_r.at[0], {"sub": other})

    picked = []
    owner = lax.rem(front[c, r], R)
    for ch in range(CH):
        for d in near_first:
            k = ch * R + d
            arrived(wrecv[ch].at[d], w_s.at[k], w_r.at[k])
        picked.append(wrecv[ch][lax.rem(r - owner + R, R)])
    cross_out[...] = -dot3(split(jnp.concatenate(picked, axis=1)), inv_pair)

    for d in near_first:
        block = gall.at[s, rowat(-d)]
        arrived(block, g_s.at[d], g_r.at[d])
        send(block, block, gs_s.at[d], gs_r.at[d], {"sub": other})
    for d in range(R):
        arrived(gall.at[other, rowat(-d)], gs_s.at[d], gs_r.at[d])
    diag_out[...] = dot3(inv_pair, split(gall[...].reshape(2 * half, width)), ((0,), (0,)))

    for cond, done in started:
        when(cond, done)


def per_device(R, C, sigma_parent, panel, diag_factor, frontier):
    half, width = panel.shape[2:]
    par_rows, par_cols = sigma_parent.shape[0], sigma_parent.shape[3]
    front_len = frontier.shape[1]
    parent = sigma_parent.reshape(par_rows, half, par_cols, width)
    parent = parent.transpose(2, 0, 1, 3).reshape(par_cols, par_rows * half, width)
    vm = pltpu.VMEM
    dma = pltpu.SemaphoreType.DMA
    side = max(C - 1, 1)
    piece = half // R
    wide = width // CH
    keys = 2 * R * CH
    scratch = (
        [vm((front_len, 2, half, wide), F32) for _ in range(C * CH)]
        + [vm((par_rows, half, wide), F32) for _ in range(CH)]
        + [vm((R, half, wide), F32) for _ in range(2 * CH)]
        + [
            vm((par_cols, par_rows * half, width), BF16),
            vm((par_cols, par_rows * half, width), BF16),
            vm((width, width), BF16),
            vm((width, width), BF16),
            vm((side * CH, par_rows, half, wide), F32),
            vm((side * CH, par_rows, half, wide), F32),
            vm((CH, 2, half, wide), F32),
            vm((CH, half, wide), F32),
            vm((CH, R, piece, wide), F32),
            vm((CH, R, piece, wide), F32),
            vm((2, R, piece, width), F32),
        ]
        + [dma((keys,))] * 2 + [dma((side * keys,))] * 2 + [dma((C * keys,))] * 2
        + [dma((side * CH,))] * 2 + [dma((CH * R,))] * 2 + [dma((CH,))] * 2 + [dma((CH * R,))] * 2
        + [dma((R,))] * 4
    )
    spec = pl.BlockSpec(memory_space=pltpu.VMEM)
    cross, diag = pl.pallas_call(
        functools.partial(kernel, R, C),
        out_shape=(jax.ShapeDtypeStruct((half, width), F32), jax.ShapeDtypeStruct((width, width), F32)),
        in_specs=[pl.BlockSpec(memory_space=pltpu.SMEM), spec, spec, spec],
        out_specs=(spec, spec),
        scratch_shapes=scratch,
        compiler_params=pltpu.CompilerParams(
            collective_id=0, has_side_effects=True, vmem_limit_bytes=(24 if C == 2 else 58) * 2**20
        ),
    )(frontier, parent, panel.reshape(half, width), diag_factor.reshape(width, width))
    return cross.reshape(panel.shape), diag.reshape(diag_factor.shape)


def solution(mesh):
    in_specs = (
        P("grp", "row", "sub", None, "col", None),
        P(("grp", "col"), "row", "sub", None),
        P(("grp", "col"), None, None),
        P("grp", None),
    )
    out_specs = (P(("grp", "col"), "row", "sub", None), P(("grp", "col"), None, None))
    return jax.shard_map(
        functools.partial(per_device, mesh.shape["row"], mesh.shape["col"]),
        mesh=mesh, in_specs=in_specs, out_specs=out_specs, check_vma=False,
    )
```

```python
import functools
import jax
import jax.numpy as jnp
from jax import lax
from jax.experimental import pallas as pl
from jax.experimental.pallas import tpu as pltpu
from jax.sharding import PartitionSpec as P

HIGHEST = lax.Precision.HIGHEST
MESH = pl.DeviceIdType.MESH
F32 = jnp.float32
BF16 = jnp.bfloat16


def split(x):
    hi = x.astype(BF16)
    return hi, (x - hi.astype(F32)).astype(BF16)


def dot3(a, b, dims=((1,), (0,))):
    def one(x, y):
        return lax.dot_general(x, y, (dims, ((), ())), preferred_element_type=F32)

    return one(a[0], b[0]) + (one(a[0], b[1]) + one(a[1], b[0]))


def dot6(a, b):
    return jnp.dot(a, b, precision=HIGHEST, preferred_element_type=F32)


def invert_steps(tri):
    size = tri.shape[0]
    row = lax.broadcasted_iota(jnp.int32, (size, size), 0)
    col = lax.broadcasted_iota(jnp.int32, (size, size), 1)
    on_diag = row == col
    only = jnp.where(on_diag, tri, 0.0)
    by_col = 1.0 / jnp.sum(only, axis=0, keepdims=True)
    by_row = 1.0 / jnp.sum(only, axis=1, keepdims=True)

    def below(m):
        same = (row // (2 * m)) == (col // (2 * m))
        return same & ((row // m) % 2 == 1) & ((col // m) % 2 == 0)

    inv = jnp.where(on_diag, by_row, 0.0) - jnp.where(below(1), tri * by_row * by_col, 0.0)
    yield inv
    m = 2
    while m < size:
        inv = inv - dot6(inv, dot6(jnp.where(below(m), tri, 0.0), inv))
        m *= 2
        yield inv


CH = 2


def kernel(R, C, *refs):
    refs = list(refs)
    front, parent, panel, factor, cross_out, diag_out = refs[:6]
    del refs[:6]
    pk = [[refs.pop(0) for _ in range(CH)] for _ in range(C)]
    w = [refs.pop(0) for _ in range(CH)]
    wsend = [refs.pop(0) for _ in range(CH)]
    wrecv = [refs.pop(0) for _ in range(CH)]
    (s_hi, s_lo, inv_hi, inv_lo, ysend, yrecv, macc, mrecv, mhalf, mpart, gall,
     z_s, z_r, x_s, x_r, sub_s, sub_r, y_s, y_r, w_s, w_r, ms_s, ms_r, m_s, m_r, g_s, g_r, gs_s, gs_r) = refs
    half = panel.shape[0]
    width = panel.shape[1]
    wide = width // CH
    par_rows = w[0].shape[0]
    front_len = front.shape[1]
    slots = front_len // C + 1
    piece = half // R
    r = lax.axis_index("row")
    c = lax.axis_index("col")
    s = lax.axis_index("sub")
    other = 1 - s

    def rowat(d):
        return lax.rem(r + d + R, R)

    def colat(e):
        return lax.rem(c + e + C, C)

    barrier = pltpu.get_barrier_semaphore()
    for d in range(1, R):
        pl.semaphore_signal(barrier, inc=1, device_id={"row": rowat(d)}, device_id_type=MESH)
    for e in range(1, C):
        pl.semaphore_signal(barrier, inc=1, device_id={"col": colat(e)}, device_id_type=MESH)
    pl.semaphore_signal(barrier, inc=1, device_id={"sub": other}, device_id_type=MESH)
    pl.semaphore_wait(barrier, R - 1 + C - 1 + 1)

    started = []

    def remote(src, dst, ssem, rsem, dev):
        return pltpu.make_async_remote_copy(
            src_ref=src, dst_ref=dst, send_sem=ssem, recv_sem=rsem, device_id=dev, device_id_type=MESH
        )

    def send(src, dst, ssem, rsem, dev, cond=None):
        def go():
            remote(src, dst, ssem, rsem, dev).start()

        def done():
            remote(src, dst, ssem, rsem, dev).wait_send()

        when(cond, go)
        started.append((cond, done))

    def when(cond, body):
        if cond is None:
            body()
        else:
            pl.when(cond)(body)

    def arrived(dst, ssem, rsem):
        remote(dst, dst, ssem, rsem, {"sub": other}).wait_recv()

    far_first = sorted(range(1, R), key=lambda d: abs(d - R / 2))
    near_first = far_first[::-1]

    def key(way, t, ch):
        return (way * R + t) * CH + ch

    keys = 2 * R * CH

    def source(way, t):
        return r - t if way == 0 else r + t

    def from_row(way, t):
        if t == 0:
            return None
        return r >= t if way == 0 else r + t <= R - 1

    def both(a, b):
        return b if a is None else a & b

    def pass_on(way, t, ch):
        here = from_row(way, t)
        block = pk[0][ch].at[source(way, t), s]
        if t + 1 < R:
            for side in (0, 1) if t == 0 else (way,):
                k = key(side, t + 1, ch)
                inside = r < R - 1 if side == 0 else r > 0
                send(block, block, z_s.at[k], z_r.at[k], {"row": r + 1 if side == 0 else r - 1}, both(here, inside))
        k = key(way, t, ch)
        for e in range(1, C):
            q = (e - 1) * keys + k
            send(block, pk[e][ch].at[source(way, t), s], x_s.at[q], x_r.at[q], {"col": colat(e)}, here)
        send(block, block, sub_s.at[k], sub_r.at[k], {"sub": other}, here)

    def take_row(way, t, ch):
        k = key(way, t, ch)
        when(from_row(way, t), lambda: arrived(pk[0][ch].at[source(way, t), s], z_s.at[k], z_r.at[k]))
        pass_on(way, t, ch)

    def take_col(e, way, t, ch):
        q = (e - 1) * keys + key(way, t, ch)
        here = from_row(way, t)
        block = pk[e][ch].at[source(way, t), s]
        when(here, lambda: arrived(block, x_s.at[q], x_r.at[q]))
        q += keys
        send(block, block, sub_s.at[q], sub_r.at[q], {"sub": other}, here)

    def take_sub(e, way, t, ch):
        q = e * keys + key(way, t, ch)
        when(from_row(way, t), lambda: arrived(pk[e][ch].at[source(way, t), other], sub_s.at[q], sub_r.at[q]))

    h = width // 2
    tri = factor[...]
    steps = [invert_steps(tri[:h, :h]), invert_steps(tri[h:, h:])]
    blocks = [None, None]

    def advance(count=1):
        for _ in range(count):
            for i in range(2):
                blocks[i] = next(steps[i], blocks[i])

    for ch in range(CH):
        pk[0][ch][r, s] = panel[:, ch * wide : (ch + 1) * wide]
        pass_on(0, 0, ch)

    for j in range(parent.shape[0]):
        hi, lo = split(parent[j])
        s_hi[j] = hi
        s_lo[j] = lo

    for t in range(1, R):
        for ch in range(CH):
            take_row(0, t, ch)
            take_row(1, t, ch)
        for ch in range(CH):
            for e in range(1, C):
                for way in (0,) if t == 1 else (0, 1):
                    take_col(e, way, t - 1, ch)
        if t < 3:
            advance()

    def product(e, ch):
        kid = colat(-e)
        count = jnp.int32(0)
        which = [jnp.int32(0)] * slots
        column = [jnp.int32(0)] * slots
        for b in range(front_len):
            f = front[kid, b]
            hit = lax.rem(f, C) == c
            for m in range(slots):
                here = hit & (count == m)
                which[m] = jnp.where(here, b, which[m])
                column[m] = jnp.where(here, lax.div(f, C), column[m])
            count = count + hit.astype(jnp.int32)
        total = None
        for m in range(slots):
            used = jnp.where(count > m, 1.0, 0.0).astype(F32)
            block = pk[e][ch][which[m]].reshape(2 * half, wide) * used
            term = dot3((s_hi[column[m]], s_lo[column[m]]), split(block))
            total = term if total is None else total + term
        return total.reshape(par_rows, half, wide)

    ways = [(0, 0)] + [(way, t) for t in range(1, R) for way in (0, 1)]
    for ch in range(CH):
        for e in range(1, C):
            for way in (0, 1):
                take_col(e, way, R - 1, ch)
        for e in range(1, C):
            for way, t in ways:
                take_sub(e, way, t, ch)
            n = (e - 1) * CH + ch
            ysend[n] = product(e, ch)
            send(ysend.at[n], yrecv.at[n], y_s.at[n], y_r.at[n], {"col": colat(-e)})
    for ch in range(CH):
        for way, t in ways:
            take_sub(0, way, t, ch)
    for ch in range(CH):
        w[ch][...] = product(0, ch)

    lhs = []
    for p in range(par_rows):
        which = jnp.int32(0)
        used = jnp.float32(0.0)
        for a in range(front_len):
            here = front[c, a] == p * R + r
            which = jnp.where(here, a, which)
            used = jnp.where(here, 1.0, used)
        lhs.append(jnp.concatenate([pk[0][ch][which, s] for ch in range(CH)], axis=1) * used)
    lhs = split(jnp.concatenate(lhs, axis=0))

    advance(8)
    top, low = blocks
    corner = -dot6(low, dot6(tri[h:, :h], top))
    inverse = jnp.concatenate(
        [jnp.concatenate([top, jnp.zeros((h, h), F32)], axis=1), jnp.concatenate([corner, low], axis=1)], axis=0
    )
    hi, lo = split(inverse)
    inv_hi[...] = hi
    inv_lo[...] = lo
    inv_pair = (inv_hi[...], inv_lo[...])

    def rows_out(ch):
        for e in range(1, C):
            n = (e - 1) * CH + ch
            arrived(yrecv.at[n], y_s.at[n], y_r.at[n])
            w[ch][...] = w[ch][...] + yrecv[n]
        macc[ch] = dot3(lhs, split(w[ch][...].reshape(par_rows * half, wide)), ((0,), (0,))).reshape(2, half, wide)
        send(macc.at[ch, other], mrecv.at[ch], ms_s.at[ch], ms_r.at[ch], {"sub": other})
        for d in range(R):
            wsend[ch][d] = w[ch][lax.div(front[c, rowat(d)], R)]

    def rows_send(ch):
        for d in far_first:
            if d:
                k = ch * R + d
                send(wsend[ch].at[d], wrecv[ch].at[d], w_s.at[k], w_r.at[k], {"row": rowat(d)})
        wrecv[ch][0] = wsend[ch][0]

    def diag_out_part(ch):
        arrived(mrecv.at[ch], ms_s.at[ch], ms_r.at[ch])
        mhalf[ch] = (macc[ch, s] + mrecv[ch]).reshape(R, piece, wide)
        for d in far_first:
            k = ch * R + d
            send(mhalf.at[ch, rowat(d)], mpart.at[ch, d], m_s.at[k], m_r.at[k], {"row": rowat(d)})

    for ch in range(CH):
        rows_out(ch)
        if ch == 0:
            rows_send(ch)
        diag_out_part(ch)
        if ch:
            rows_send(ch)

    total = []
    for ch in range(CH):
        part = mhalf[ch, r]
        for d in near_first:
            k = ch * R + d
            arrived(mpart.at[ch, d], m_s.at[k], m_r.at[k])
            part = part + mpart[ch, d]
        total.append(part)
    total = jnp.concatenate(total, axis=1)
    row = lax.broadcasted_iota(jnp.int32, (piece, width), 0) + (s * half + r * piece)
    col = lax.broadcasted_iota(jnp.int32, (piece, width), 1)
    total = total + jnp.where(row == col, 1.0, 0.0)
    gall[s, r] = dot3(split(total), inv_pair)
    mine = gall.at[s, r]
    for d in far_first:
        send(mine, mine, g_s.at[d], g_r.at[d], {"row": rowat(d)})
    send(mine, mine, gs_s.at[0], gs_r.at[0], {"sub": other})

    picked = []
    owner = lax.rem(front[c, r], R)
    for ch in range(CH):
        for d in near_first:
            k = ch * R + d
            arrived(wrecv[ch].at[d], w_s.at[k], w_r.at[k])
        picked.append(wrecv[ch][lax.rem(r - owner + R, R)])
    cross_out[...] = -dot3(split(jnp.concatenate(picked, axis=1)), inv_pair)

    for d in near_first:
        block = gall.at[s, rowat(-d)]
        arrived(block, g_s.at[d], g_r.at[d])
        send(block, block, gs_s.at[d], gs_r.at[d], {"sub": other})
    for d in range(R):
        arrived(gall.at[other, rowat(-d)], gs_s.at[d], gs_r.at[d])
    diag_out[...] = dot3(inv_pair, split(gall[...].reshape(2 * half, width)), ((0,), (0,)))

    for cond, done in started:
        when(cond, done)


def per_device(R, C, sigma_parent, panel, diag_factor, frontier):
    half, width = panel.shape[2:]
    par_rows, par_cols = sigma_parent.shape[0], sigma_parent.shape[3]
    front_len = frontier.shape[1]
    parent = sigma_parent.reshape(par_rows, half, par_cols, width)
    parent = parent.transpose(2, 0, 1, 3).reshape(par_cols, par_rows * half, width)
    vm = pltpu.VMEM
    dma = pltpu.SemaphoreType.DMA
    side = max(C - 1, 1)
    piece = half // R
    wide = width // CH
    keys = 2 * R * CH
    scratch = (
        [vm((front_len, 2, half, wide), F32) for _ in range(C * CH)]
        + [vm((par_rows, half, wide), F32) for _ in range(CH)]
        + [vm((R, half, wide), F32) for _ in range(2 * CH)]
        + [
            vm((par_cols, par_rows * half, width), BF16),
            vm((par_cols, par_rows * half, width), BF16),
            vm((width, width), BF16),
            vm((width, width), BF16),
            vm((side * CH, par_rows, half, wide), F32),
            vm((side * CH, par_rows, half, wide), F32),
            vm((CH, 2, half, wide), F32),
            vm((CH, half, wide), F32),
            vm((CH, R, piece, wide), F32),
            vm((CH, R, piece, wide), F32),
            vm((2, R, piece, width), F32),
        ]
        + [dma((keys,))] * 2 + [dma((side * keys,))] * 2 + [dma((C * keys,))] * 2
        + [dma((side * CH,))] * 2 + [dma((CH * R,))] * 2 + [dma((CH,))] * 2 + [dma((CH * R,))] * 2
        + [dma((R,))] * 4
    )
    spec = pl.BlockSpec(memory_space=pltpu.VMEM)
    cross, diag = pl.pallas_call(
        functools.partial(kernel, R, C),
        out_shape=(jax.ShapeDtypeStruct((half, width), F32), jax.ShapeDtypeStruct((width, width), F32)),
        in_specs=[pl.BlockSpec(memory_space=pltpu.SMEM), spec, spec, spec],
        out_specs=(spec, spec),
        scratch_shapes=scratch,
        compiler_params=pltpu.CompilerParams(
            collective_id=0, has_side_effects=True, vmem_limit_bytes=(24 if C == 2 else 58) * 2**20
        ),
    )(frontier, parent, panel.reshape(half, width), diag_factor.reshape(width, width))
    return cross.reshape(panel.shape), diag.reshape(diag_factor.shape)


def solution(mesh):
    in_specs = (
        P("grp", "row", "sub", None, "col", None),
        P(("grp", "col"), "row", "sub", None),
        P(("grp", "col"), None, None),
        P("grp", None),
    )
    out_specs = (P(("grp", "col"), "row", "sub", None), P(("grp", "col"), None, None))
    return jax.shard_map(
        functools.partial(per_device, mesh.shape["row"], mesh.shape["col"]),
        mesh=mesh, in_specs=in_specs, out_specs=out_specs, check_vma=False,
    )
```
